128 devices in a mesh: role: 2 (over core), dev: 64 (over z, y, x).
Axes of the slice: x: 4, y: 4, z: 4, core: 2. Of those that a mesh axis runs over, the one named last changes fastest.
Arguments:
- layer_in: bfloat16 [16384, 4096], P(('role', 'dev')), may hold values from -24 to 24
- norm_gain: float32 [4096], replicated, may hold values from 0.1 to 1.9
- routes: int32 [16384, 4], P(('role', 'dev')), may hold values from 0 to 127, all different within a row; in each aligned block of 128 rows (0 to 127, 128 to 255, ...) at most 5 rows name the same one
- gate_weights: float32 [16384, 4], P(('role', 'dev')), may hold values from 0.05 to 1
- out_grad: bfloat16 [16384, 4096], P(('role', 'dev')), may hold values from -6 to 6
- expert_gate_up: bfloat16 [128, 4096, 1536], P(('role', 'dev')), may hold values from -0.09375 to 0.09375
- expert_down: bfloat16 [128, 768, 4096], P(('role', 'dev')), may hold values from -0.21875 to 0.21875
Outputs:
- layer_out: bfloat16 [16384, 4096], P(('role', 'dev'))
- input_grad: bfloat16 [16384, 4096], P(('role', 'dev'))
- gate_grad: float32 [16384, 4], P(('role', 'dev'))
- gain_grad: float32 [4096], P(('role', 'dev'))
The draws below stay inside these ranges and needn't reach their ends.
Inputs may be any that keep to these rules, and one draw needn't show every extreme that they name: `routes`: each row names 4 different experts. Among the 128 rows of one device no expert is named more than 5 times, a bound that some block reaches.
All inputs are finite; a program needn't handle non-finite values.
Results may differ from the reference program's by a relative error of at most 0.0065.
Values may be sent and summed in bfloat16 or wider, within the bound.
No kernel may reach another device: no remote copies, remote signals or barrier semaphores. Data moves between devices by JAX's collectives and lax.ppermute only.
A program may use at most 192 MiB of HBM per device.

```python
import math
import jax
import jax.numpy as jnp
import numpy as np
from jax import lax

D = 4096
FF = 768
K = 4
TOK_DEV = 128
EXPERTS = 128
TOKENS = 16384
CAP = 5


def strengthened(array, key, source, target, shards_of, factor):
    owner, partner = [(jnp.arange(array.shape[dim]) // (array.shape[dim] // shards_of)).reshape([-1 if axis == dim else 1 for axis in range(array.ndim)]) for dim in (source, target)]
    chosen = jax.random.permutation(key, shards_of)[partner]
    strong = (owner == chosen) | (owner == (partner + shards_of // 2) % shards_of)
    return jnp.where(strong, factor * array, array)


def steps_of(rng, dims, cuts, low, high):
    level, own = 1.0, jax.random.fold_in(rng, 6)
    for axis_at, blocks in cuts:
        steps = jnp.exp(jax.random.uniform(jax.random.fold_in(own, axis_at), (blocks,), jnp.float32, low / len(cuts), high / len(cuts)))
        level = level * jnp.repeat(steps, dims[axis_at] // blocks).reshape([-1 if axis == axis_at else 1 for axis in range(len(dims))])
    return level


def routed_block(key, own, number, rows, number_of, top, limit, slope):
    order = jax.random.permutation(key, number_of)
    crowded, ordinary = load_shares(number_of, rows * top, limit, slope, True), load_shares(number_of, rows * top, limit, slope, False)
    places = jnp.arange(number_of)

    def named(sizes, turn):
        used = int((sizes > 0).sum())
        fixed = max(1, used // 4)
        passed = fixed + (places - fixed + turn * (used - fixed)) % max(1, number_of - fixed)
        return jnp.zeros((number_of,), jnp.int32).at[order[jnp.where(places < fixed, places, passed)]].set(jnp.asarray(sizes, jnp.int32))

    sizes = jnp.where(number % 4 == 0, named(crowded, number // 4), named(ordinary, number - number // 4 - 1))
    mixed = jax.random.permutation(jax.random.fold_in(own, 3), number_of)
    source_of, taker = mixed[0:number_of // 2 * 2:2], mixed[1:number_of // 2 * 2:2]
    room = jnp.minimum(sizes[source_of] - 1, limit - sizes[taker]) // 2
    room = jnp.where((source_of == order[0]) | (taker == order[0]) | (sizes[taker] == 0), 0, jnp.maximum(room, 0))
    passed = jax.random.randint(jax.random.fold_in(own, 4), (number_of // 2,), 0, 1 << 20) % (room + 1)
    sizes = sizes.at[source_of].add(-passed).at[taker].add(passed)
    members = jnp.searchsorted(jnp.cumsum(sizes), jnp.arange(rows * top), side="right").astype(jnp.int32)
    table = members.reshape(top, rows).T
    table = table[jax.random.permutation(jax.random.fold_in(own, 1), rows)]
    turn = jax.random.randint(jax.random.fold_in(own, 2), (rows, 1), 0, top)
    return jnp.take_along_axis(table, (jnp.arange(top)[None, :] + turn) % top, axis=1)


def load_shares(count, total, bound, lean, full):
    portions = [(1 << 20) // math.isqrt(rank ** lean) + 1 for rank in range(1, count + 1)]
    largest = bound if full else min(bound, max(-(-total // count), total * portions[0] // sum(portions)))
    least = 1 if total - largest >= count - 1 else 0
    holding, surplus = [largest] + [least] * (count - 1), total - largest - least * (count - 1)
    while surplus > 0:
        free = [i for i in range(1, count) if holding[i] < largest] or [i for i in range(1, count) if holding[i] < bound]
        mass, left = sum([portions[i] for i in free]), surplus
        for i in free:
            more = min(bound - holding[i], max(1, left * portions[i] // mass), surplus)
            holding[i] = holding[i] + more
            surplus = surplus - more
    return np.array(holding)


def normal_values(stream_key, shape, scale, limit, pieces=(), kind=jnp.bfloat16):
    entries = scale * jax.random.normal(stream_key, shape, jnp.float32)
    if pieces:
        entries = entries * steps_of(stream_key, shape, pieces, -0.22, 0.18)
    return jnp.clip(entries, -limit, limit).astype(kind)


def gaussian_with(stream_key, dims, deviation, bound, pieces, heavy, held_as=jnp.bfloat16):
    values = deviation * jax.random.normal(stream_key, dims, jnp.float32)
    if pieces:
        values = values * steps_of(stream_key, dims, pieces, -0.22, 0.18)
    return jnp.clip(strengthened(values, jax.random.fold_in(stream_key, 3), *heavy), -bound, bound).astype(held_as)


def setup_inputs(seed: int = 0) -> dict:
    arg_keys = jax.random.split(jax.random.key(seed), 8)
    layer_in = gaussian_with(arg_keys[0], (TOKENS, D), 1.0, 24.0, ((0, 128),), (0, 1, 128, 5.5))
    norm_gain = jnp.clip(1.0 + 0.18 * jax.random.normal(arg_keys[1], (D,), jnp.float32), 0.1, 1.9)
    routes_keys = jax.random.split(jax.random.fold_in(arg_keys[2], 1), TOKENS // TOK_DEV)
    routes_turns = jax.random.permutation(jax.random.fold_in(arg_keys[2], 3), TOKENS // TOK_DEV)
    routes = jax.vmap(lambda own, number: routed_block(jax.random.fold_in(arg_keys[2], 2), own, number, TOK_DEV, EXPERTS, K, CAP, 2))(routes_keys, routes_turns).reshape((TOKENS, K))
    gate_weights = jnp.clip(jnp.exp(math.log(1.0) - 2.9957323 * jax.random.uniform(arg_keys[3], (TOKENS, K), jnp.float32) ** steps_of(arg_keys[3], (TOKENS, K), ((0, 128),), -0.2, 0.2)), 0.05, 1.0)
    out_grad = normal_values(arg_keys[4], (TOKENS, D), 1.0, 6.0, ((0, 128),))
    expert_gate_up = normal_values(arg_keys[5], (EXPERTS, D, 2 * FF), D ** -0.5, 0.09375, ((0, 128),))
    expert_down = normal_values(arg_keys[6], (EXPERTS, FF, D), FF ** -0.5, 0.21875, ((0, 128),))
    return {"layer_in": layer_in, "norm_gain": norm_gain, "routes": routes, "gate_weights": gate_weights, "out_grad": out_grad, "expert_gate_up": expert_gate_up, "expert_down": expert_down}


epsilon = 1e-06

def swish_parts(projected, hidden_units):
    gate_part = projected[:, :hidden_units]
    up_part = projected[:, hidden_units:]
    sigmoid_val = jax.nn.sigmoid(gate_part)
    active = gate_part * sigmoid_val
    return (gate_part, up_part, sigmoid_val, active)

def transposed(left, right):
    return lax.dot_general(left, right, (((1,), (1,)), ((), ())), preferred_element_type=jnp.float32)

def reference(layer_in, norm_gain, routes, gate_weights, out_grad, expert_gate_up, expert_down):
    residual = layer_in.astype(jnp.float32)
    token_count = residual.shape[0]
    root_mean = jnp.sqrt(lax.optimization_barrier(jnp.mean(residual * residual, axis=-1, keepdims=True)) + epsilon)
    unit_rows = residual / root_mean
    normed = (unit_rows * norm_gain).astype(jnp.bfloat16)
    pair_count = token_count * K
    flat_routes = routes.reshape(-1).astype(jnp.int32)
    one_hot = (flat_routes[:, None] == jnp.arange(EXPERTS, dtype=jnp.int32)[None, :]).astype(jnp.int32)
    blocked = one_hot.reshape(-1, TOK_DEV * K, EXPERTS)
    earlier = (jnp.cumsum(blocked, axis=1) - blocked) * blocked
    slot_of = lax.optimization_barrier(jnp.sum(earlier, axis=-1)).reshape(-1).astype(jnp.int32)
    block_of = (jnp.arange(pair_count, dtype=jnp.int32) // (TOK_DEV * K)).astype(jnp.int32)
    position = (flat_routes * (EXPERTS * CAP) + block_of * CAP + slot_of).astype(jnp.int32)
    slot_table = jnp.full((EXPERTS * EXPERTS * CAP,), pair_count, jnp.int32)
    slot_table = slot_table.at[position].set(jnp.arange(pair_count, dtype=jnp.int32)).reshape(EXPERTS, EXPERTS * CAP)
    token_table = jnp.where(slot_table < pair_count, slot_table // K, token_count).astype(jnp.int32)
    zero_row = jnp.zeros((1, D), jnp.bfloat16)
    normed_pad = jnp.concatenate([normed, zero_row], axis=0)
    grad_pad = jnp.concatenate([out_grad, zero_row], axis=0)
    weight_pad = jnp.concatenate([gate_weights.reshape(-1).astype(jnp.float32), jnp.zeros((1,), jnp.float32)])

    def per_expert(carry, inputs):
        routed_sum, normed_grad, gate_grad = carry
        slots_here, tokens_here, w_gate_up, w_down = inputs
        rows = normed_pad[tokens_here]
        projected = jnp.dot(rows, w_gate_up, preferred_element_type=jnp.float32)
        gate_part, up_part, sigmoid_val, active = swish_parts(projected, FF)
        hidden = (active * up_part).astype(jnp.bfloat16)
        expert_rows = jnp.dot(hidden, w_down, preferred_element_type=jnp.float32).astype(jnp.bfloat16)
        expert_float = expert_rows.astype(jnp.float32)
        weights = weight_pad[slots_here]
        grad_rows = grad_pad[tokens_here].astype(jnp.float32)
        routed_sum = routed_sum.at[tokens_here].add(weights[:, None] * expert_float)
        gate_grad = gate_grad.at[slots_here].set(lax.optimization_barrier(jnp.sum(grad_rows * expert_float, axis=-1)))
        scaled = (weights[:, None] * grad_rows).astype(jnp.bfloat16)
        hidden_grad = transposed(scaled, w_down)
        gate_grad_part = hidden_grad * up_part * sigmoid_val * (1.0 + gate_part * (1.0 - sigmoid_val))
        pre_grad = jnp.concatenate([gate_grad_part, hidden_grad * active], axis=-1).astype(jnp.bfloat16)
        back_rows = transposed(pre_grad, w_gate_up).astype(jnp.bfloat16)
        normed_grad = normed_grad.at[tokens_here].add(back_rows.astype(jnp.float32))
        return ((routed_sum, normed_grad, gate_grad), None)
    start = (jnp.zeros((token_count + 1, D), jnp.float32), jnp.zeros((token_count + 1, D), jnp.float32), jnp.zeros((pair_count + 1,), jnp.float32))
    (routed_sum, normed_grad, gate_grad), _ = lax.scan(per_expert, start, (slot_table, token_table, expert_gate_up, expert_down))
    routed_sum = routed_sum[:token_count]
    normed_grad = normed_grad[:token_count]
    layer_out = (residual + routed_sum).astype(jnp.bfloat16)
    gate_grad = gate_grad[:pair_count].reshape(token_count, K)
    gain_grad = lax.optimization_barrier(jnp.sum(normed_grad * unit_rows, axis=0))
    scaled_gain = normed_grad * norm_gain
    input_grad = (out_grad.astype(jnp.float32) + (scaled_gain - unit_rows * lax.optimization_barrier(jnp.mean(scaled_gain * unit_rows, axis=-1, keepdims=True))) / root_mean).astype(jnp.bfloat16)
    return (layer_out, input_grad, gate_grad, gain_grad)
```

```python
import jax
import jax.numpy as jnp
from jax import lax
from jax.experimental import pallas as pl
from jax.experimental.pallas import tpu as pltpu
from jax.sharding import PartitionSpec as P

AXES = ("role", "dev")
EPSILON = 1e-06
LANES = 128
GROUP = 16
EXTRA = 8
F32 = jnp.float32
BF16 = jnp.bfloat16
VMEM = pl.BlockSpec(memory_space=pltpu.VMEM)
SMEM = pl.BlockSpec(memory_space=pltpu.SMEM)
PARAMS = pltpu.CompilerParams(vmem_limit_bytes=40 * 1024 * 1024)


def zero_fill(ref):
    def one(i, carry):
        ref[i] = jnp.zeros(ref.shape[1:], ref.dtype)
        return carry

    lax.fori_loop(0, ref.shape[0], one, 0)


def columns_of(ref, first, piece):
    return ref[pl.ds(first, GROUP), piece * LANES : (piece + 1) * LANES].astype(F32)


def strip(group, piece, pieces):
    return pl.ds(group * GROUP * pieces + piece, GROUP, stride=pieces)


def token_rows(token, pieces):
    return pl.ds(pl.multiple_of(token * pieces, pieces), pieces)


def slot_rows(slot, pieces):
    return pl.ds(pl.multiple_of(slot * pieces, pieces), pieces)


def send_rows_kernel(routes, layer_in, gain, out, place, rows, count):
    tokens, width = layer_in.shape
    pieces = width // LANES
    top = routes.shape[0]

    def clear(i, carry):
        count[i] = 0
        return carry

    lax.fori_loop(0, count.shape[0], clear, 0)
    zero_fill(out)

    def normalise(group, carry):
        first = pl.multiple_of(group * GROUP, GROUP)
        square = jnp.zeros((GROUP, LANES), F32)
        for piece in range(pieces):
            x = columns_of(layer_in, first, piece)
            square = square + x * x
        root_mean = jnp.sqrt(jnp.sum(square, axis=-1, keepdims=True) / width + EPSILON)
        inverse = 1.0 / root_mean
        for piece in range(pieces):
            unit = columns_of(layer_in, first, piece) * inverse
            rows[strip(group, piece, pieces), :] = (
                unit * gain[:, piece * LANES : (piece + 1) * LANES]
            )
        return carry

    lax.fori_loop(0, tokens // GROUP, normalise, 0)

    def place_token(token, carry):
        row = rows[token_rows(token, pieces), :].astype(BF16)
        for k in range(top):
            expert = routes[k, token]
            slot = count[expert]
            count[expert] = slot + 1
            place[k, token] = expert * 8 + slot
            out[expert, slot_rows(slot, pieces), :] = row
        return carry

    lax.fori_loop(0, tokens, place_token, 0)


def send_grads_kernel(place, weights, out_grad, out, rows):
    tokens, width = out_grad.shape
    pieces = width // LANES
    top = place.shape[0]
    zero_fill(out)

    def spread(group, carry):
        first = pl.multiple_of(group * GROUP, GROUP)
        for piece in range(pieces):
            rows[strip(group, piece, pieces), :] = columns_of(out_grad, first, piece)
        return carry

    lax.fori_loop(0, tokens // GROUP, spread, 0)

    def place_token(token, carry):
        row = rows[token_rows(token, pieces), :]
        for k in range(top):
            where = place[k, token]
            out[where // 8, slot_rows(where % 8, pieces), :] = (row * weights[k, token]).astype(BF16)
        return carry

    lax.fori_loop(0, tokens, place_token, 0)


def outputs_kernel(place, weights, layer_in, out_grad, returned, layer_out, gate_grad, rows, sums, dots):
    tokens, width = out_grad.shape
    pieces = width // LANES
    top = place.shape[0]

    def spread(group, carry):
        first = pl.multiple_of(group * GROUP, GROUP)
        for piece in range(pieces):
            rows[strip(group, piece, pieces), :] = columns_of(out_grad, first, piece)
        return carry

    lax.fori_loop(0, tokens // GROUP, spread, 0)

    def combine(token, carry):
        grad = rows[token_rows(token, pieces), :]
        total = jnp.zeros((pieces, LANES), F32)
        for k in range(top):
            where = place[k, token]
            row = returned[where // 8, slot_rows(where % 8, pieces), :].astype(F32)
            total = total + weights[k, token] * row
            dots[k, pl.ds(token, 1), :] = jnp.sum(row * grad, axis=0, keepdims=True)
        sums[token_rows(token, pieces), :] = total
        return carry

    lax.fori_loop(0, tokens, combine, 0)
    for k in range(top):
        gate_grad[k : k + 1, :] = jnp.sum(dots[k].T, axis=0, keepdims=True)

    def finish(group, carry):
        first = pl.multiple_of(group * GROUP, GROUP)
        for piece in range(pieces):
            x = columns_of(layer_in, first, piece)
            layer_out[pl.ds(first, GROUP), piece * LANES : (piece + 1) * LANES] = (
                x + sums[strip(group, piece, pieces), :]
            ).astype(BF16)
        return carry

    lax.fori_loop(0, tokens // GROUP, finish, 0)


def input_grad_kernel(place, layer_in, gain, out_grad, returned, input_grad, gain_grad, sums):
    tokens, width = out_grad.shape
    pieces = width // LANES
    top = place.shape[0]
    peers = returned.shape[0]
    body_rows = returned.shape[1] - EXTRA

    def combine(token, carry):
        total = jnp.zeros((pieces, LANES), F32)
        for k in range(top):
            where = place[k, token]
            total = total + returned[where // 8, slot_rows(where % 8, pieces), :].astype(F32)
        sums[token_rows(token, pieces), :] = total
        return carry

    lax.fori_loop(0, tokens, combine, 0)

    def finish(group, carry):
        first = pl.multiple_of(group * GROUP, GROUP)
        square = jnp.zeros((GROUP, LANES), F32)
        along = jnp.zeros((GROUP, LANES), F32)
        for piece in range(pieces):
            x = columns_of(layer_in, first, piece)
            q = sums[strip(group, piece, pieces), :] * gain[:, piece * LANES : (piece + 1) * LANES]
            square = square + x * x
            along = along + q * x
        inverse = 1.0 / jnp.sqrt(jnp.sum(square, axis=-1, keepdims=True) / width + EPSILON)
        mean = jnp.sum(along, axis=-1, keepdims=True) * inverse / width
        for piece in range(pieces):
            cut = slice(piece * LANES, (piece + 1) * LANES)
            unit = columns_of(layer_in, first, piece) * inverse
            q = sums[strip(group, piece, pieces), :] * gain[:, cut]
            input_grad[pl.ds(first, GROUP), cut] = (
                columns_of(out_grad, first, piece) + (q - unit * mean) * inverse
            ).astype(BF16)
        return carry

    lax.fori_loop(0, tokens // GROUP, finish, 0)

    def add_peer(peer, total):
        return total + returned[peer, body_rows : body_rows + EXTRA, :].astype(F32)

    gain_grad[...] = lax.fori_loop(0, peers, add_peer, jnp.zeros((EXTRA, LANES), F32))


def transposed(left, right):
    return lax.dot_general(left, right, (((1,), (1,)), ((), ())), preferred_element_type=F32)


def exchange(buffer):
    return lax.all_to_all(buffer, AXES, split_axis=0, concat_axis=0, tiled=True)


def three_parts(values):
    high = lax.reduce_precision(values, 8, 7)
    middle = lax.reduce_precision(values - high, 8, 7)
    low = values - high - middle
    return high.astype(BF16), middle.astype(BF16), low.astype(BF16)


def body(layer_in, norm_gain, routes, gate_weights, out_grad, expert_gate_up, expert_down):
    tokens, width = layer_in.shape
    top = routes.shape[1]
    peers = lax.axis_size(AXES)
    slots = tokens * top * 5 // (4 * peers)
    pieces = width // LANES
    hidden_units = expert_down.shape[1]
    row_count = peers * slots
    block = (peers, slots * pieces, LANES)
    gain = norm_gain.reshape(1, width)
    by_choice = routes.T
    weights = gate_weights.T
    token_scratch = pltpu.VMEM((tokens * pieces, LANES), F32)

    send_rows, place = pl.pallas_call(
        send_rows_kernel,
        out_shape=(
            jax.ShapeDtypeStruct(block, BF16),
            jax.ShapeDtypeStruct((top, tokens), jnp.int32),
        ),
        in_specs=[SMEM, VMEM, VMEM],
        out_specs=(VMEM, SMEM),
        scratch_shapes=[token_scratch, pltpu.SMEM((peers,), jnp.int32)],
        compiler_params=PARAMS,
        name="send_rows",
    )(by_choice, layer_in, gain)
    arrived = exchange(send_rows).reshape(row_count, pieces, LANES).reshape(row_count, width)

    send_grads = pl.pallas_call(
        send_grads_kernel,
        out_shape=jax.ShapeDtypeStruct(block, BF16),
        in_specs=[SMEM, SMEM, VMEM],
        out_specs=VMEM,
        scratch_shapes=[token_scratch],
        compiler_params=PARAMS,
        name="send_grads",
    )(place, weights, out_grad)
    grad_rows = exchange(send_grads).reshape(row_count, pieces, LANES).reshape(row_count, width)

    w_gate_up = expert_gate_up[0]
    w_down = expert_down[0]
    projected = jnp.dot(arrived, w_gate_up, preferred_element_type=F32)
    g = projected[:, :hidden_units]
    u = projected[:, hidden_units:]
    s = jax.nn.sigmoid(g)
    active = g * s
    hidden = (active * u).astype(BF16)
    expert_rows = jnp.dot(hidden, w_down, preferred_element_type=F32).astype(BF16)
    returned = exchange(expert_rows.reshape(row_count, pieces, LANES).reshape(block))

    hidden_grad = transposed(grad_rows, w_down)
    gate_part = hidden_grad * u * s * (1.0 + g * (1.0 - s))
    pre_grad = jnp.concatenate([gate_part, hidden_grad * active], axis=-1).astype(BF16)
    back_rows = transposed(pre_grad, w_gate_up).astype(BF16)
    terms = jnp.sum(back_rows.astype(F32) * arrived.astype(F32), axis=0) / norm_gain
    share = width // peers
    parts = jnp.concatenate([p.reshape(peers, share) for p in three_parts(terms)], axis=-1)
    parts = jnp.pad(parts[:, None, :], ((0, 0), (0, EXTRA - 1), (0, LANES - 3 * share)))
    send_back = jnp.concatenate(
        [back_rows.reshape(row_count, pieces, LANES).reshape(block), parts], axis=1
    )
    came_back = exchange(send_back)

    layer_out, gate_grad = pl.pallas_call(
        outputs_kernel,
        out_shape=(
            jax.ShapeDtypeStruct((tokens, width), BF16),
            jax.ShapeDtypeStruct((top, tokens), F32),
        ),
        in_specs=[SMEM, SMEM, VMEM, VMEM, VMEM],
        out_specs=(VMEM, VMEM),
        scratch_shapes=[token_scratch, token_scratch, pltpu.VMEM((top, tokens, LANES), F32)],
        compiler_params=PARAMS,
        name="outputs",
    )(place, weights, layer_in, out_grad, returned)

    input_grad, gain_sums = pl.pallas_call(
        input_grad_kernel,
        out_shape=(
            jax.ShapeDtypeStruct((tokens, width), BF16),
            jax.ShapeDtypeStruct((EXTRA, LANES), F32),
        ),
        in_specs=[SMEM, VMEM, VMEM, VMEM, VMEM],
        out_specs=(VMEM, VMEM),
        scratch_shapes=[token_scratch],
        compiler_params=PARAMS,
        name="input_grad",
    )(place, layer_in, gain, out_grad, came_back)
    gain_grad = jnp.sum(gain_sums[0, : 3 * share].reshape(3, share), axis=0)
    return (layer_out, input_grad, gate_grad.T, gain_grad)


def solution(mesh):
    split = P(AXES, None)
    in_specs = (split, P(), split, split, split, P(AXES, None, None), P(AXES, None, None))
    out_specs = (split, split, split, P(AXES))
    return jax.shard_map(body, mesh=mesh, in_specs=in_specs, out_specs=out_specs, check_vma=False)
```

```python
import functools

import jax
import jax.numpy as jnp
from jax import lax
from jax.experimental import pallas as pl
from jax.experimental.pallas import tpu as pltpu
from jax.sharding import PartitionSpec as P

AXES = ("role", "dev")
EPSILON = 1e-06
LANES = 128
GROUP = 16
EXTRA = 8
F32 = jnp.float32
BF16 = jnp.bfloat16
VMEM = pl.BlockSpec(memory_space=pltpu.VMEM)
SMEM = pl.BlockSpec(memory_space=pltpu.SMEM)
HBM = pl.BlockSpec(memory_space=pltpu.HBM)
PARAMS = pltpu.CompilerParams(vmem_limit_bytes=40 * 1024 * 1024)
WHOLE = pltpu.CompilerParams(vmem_limit_bytes=60 * 1024 * 1024)


def zero_fill(ref):
    def one(i, carry):
        ref[i] = jnp.zeros(ref.shape[1:], ref.dtype)
        return carry

    lax.fori_loop(0, ref.shape[0], one, 0)


def columns_of(ref, first, piece):
    return ref[pl.ds(first, GROUP), piece * LANES : (piece + 1) * LANES].astype(F32)


def strip(group, piece, pieces):
    return pl.ds(group * GROUP * pieces + piece, GROUP, stride=pieces)


def token_rows(token, pieces):
    return pl.ds(pl.multiple_of(token * pieces, pieces), pieces)


def slot_rows(slot, pieces):
    return pl.ds(pl.multiple_of(slot * pieces, pieces), pieces)


def send_rows_kernel(
    chip_count, routes_in, layer_in, gain, out, place_out, inverse_out,
    routes, x, gain_row, spread, packed, staged, inverses, place, count, table, in_sems, out_sems,
):
    tokens, width = layer_in.shape
    pieces = width // LANES
    top = routes.shape[0]
    peers = out.shape[0]
    slots = out.shape[1] // pieces
    cores = peers // chip_count
    in_parts, out_parts = in_sems.shape[0] - 2, out_sems.shape[0] - 2
    part = tokens // in_parts
    copies = []
    for i in range(in_parts):
        cut = pl.ds(i * part, part)
        copies.append(pltpu.make_async_copy(layer_in.at[cut], x.at[cut], in_sems.at[i]))
    gain_copy = pltpu.make_async_copy(gain, gain_row, in_sems.at[in_parts])
    routes_copy = pltpu.make_async_copy(routes_in, routes, in_sems.at[in_parts + 1])
    copies[0].start()
    gain_copy.start()
    routes_copy.start()
    for copy in copies[1:]:
        copy.start()

    def clear(chip, carry):
        for core in range(cores):
            first = (chip * cores + core) * 8
            count[core * chip_count + chip] = first
            for slot in range(slots):
                table[first + slot] = tokens
        return carry

    lax.fori_loop(0, chip_count, clear, 0)
    packed[pl.ds(tokens * pieces, pieces), :] = jnp.zeros((pieces, LANES), BF16)
    routes_copy.wait()
    gain_copy.wait()

    def take_part(first):
        groups = range(first, first + part, GROUP)
        for at in groups:
            square = jnp.zeros((GROUP, LANES), F32)
            for piece in range(pieces):
                values = columns_of(x, at, piece)
                square = square + values * values
            root_mean = jnp.sqrt(jnp.sum(square, axis=-1, keepdims=True) / width + EPSILON)
            inverses[pl.ds(at, GROUP), :] = jnp.broadcast_to(1.0 / root_mean, (GROUP, LANES))
        for at in groups:
            inverse = inverses[pl.ds(at, GROUP), :]
            for piece in range(pieces):
                unit = columns_of(x, at, piece) * inverse
                spread[pl.ds((at - first) * pieces + piece, GROUP, stride=pieces), :] = (
                    unit * gain_row[:, piece * LANES : (piece + 1) * LANES]
                )
        packed[first * pieces : (first + part) * pieces, :] = spread[...].astype(BF16)
        for token in range(first, first + part):
            experts = [routes[k, token] for k in range(top)]
            wheres = [count[expert] for expert in experts]
            for k in range(top):
                count[experts[k]] = wheres[k] + 1
                place[k, token] = wheres[k]
                table[wheres[k]] = token

    for i in range(in_parts):
        copies[i].wait()
        take_part(i * part)
    sent = [
        pltpu.make_async_copy(place, place_out, out_sems.at[out_parts]),
        pltpu.make_async_copy(inverses, inverse_out, out_sems.at[out_parts + 1]),
    ]
    for copy in sent:
        copy.start()
    step = peers // out_parts

    def fill(pair, carry):
        for i in range(2):
            peer = pair * 2 + i
            chosen = [table[peer * 8 + slot] for slot in range(slots)]
            for slot in range(slots):
                staged[peer, slot * pieces : (slot + 1) * pieces, :] = packed[
                    token_rows(chosen[slot], pieces), :
                ]
        return carry

    for i in range(out_parts):
        lax.fori_loop(i * step // 2, (i + 1) * step // 2, fill, 0)
        cut = pl.ds(i * step, step)
        sent.append(pltpu.make_async_copy(staged.at[cut], out.at[cut], out_sems.at[i]))
        sent[-1].start()
    for copy in sent:
        copy.wait()


def send_grads_kernel(place, weights, out_grad, out, rows):
    tokens, width = out_grad.shape
    pieces = width // LANES
    top = place.shape[0]
    zero_fill(out)

    def spread(group, carry):
        first = pl.multiple_of(group * GROUP, GROUP)
        for piece in range(pieces):
            rows[strip(group, piece, pieces), :] = columns_of(out_grad, first, piece)
        return carry

    lax.fori_loop(0, tokens // GROUP, spread, 0)

    def place_token(token, carry):
        row = rows[token_rows(token, pieces), :]
        for k in range(top):
            where = place[k, token]
            out[where >> 3, slot_rows(where & 7, pieces), :] = (row * weights[k, token]).astype(BF16)
        return carry

    lax.fori_loop(0, tokens, place_token, 0)


def outputs_kernel(place, weights, layer_in, out_grad, returned, layer_out, gate_grad, rows, sums, dots):
    tokens, width = out_grad.shape
    pieces = width // LANES
    top = place.shape[0]

    def spread(group, carry):
        first = pl.multiple_of(group * GROUP, GROUP)
        for piece in range(pieces):
            rows[strip(group, piece, pieces), :] = columns_of(out_grad, first, piece)
        return carry

    lax.fori_loop(0, tokens // GROUP, spread, 0)

    def combine(token, carry):
        grad = rows[token_rows(token, pieces), :]
        total = jnp.zeros((pieces, LANES), F32)
        for k in range(top):
            where = place[k, token]
            row = returned[where >> 3, slot_rows(where & 7, pieces), :].astype(F32)
            total = total + weights[k, token] * row
            dots[k, pl.ds(token, 1), :] = jnp.sum(row * grad, axis=0, keepdims=True)
        sums[token_rows(token, pieces), :] = total
        return carry

    lax.fori_loop(0, tokens, combine, 0)
    for k in range(top):
        gate_grad[k : k + 1, :] = jnp.sum(dots[k].T, axis=0, keepdims=True)

    def finish(group, carry):
        first = pl.multiple_of(group * GROUP, GROUP)
        for piece in range(pieces):
            x = columns_of(layer_in, first, piece)
            layer_out[pl.ds(first, GROUP), piece * LANES : (piece + 1) * LANES] = (
                x + sums[strip(group, piece, pieces), :]
            ).astype(BF16)
        return carry

    lax.fori_loop(0, tokens // GROUP, finish, 0)


def input_grad_kernel(
    place_in, layer_in, inverse_in, gain_in, out_grad, returned, input_grad, gain_grad,
    place, x, inverse, gain_rows, grad, held, units, sums, dots, result, in_sems, sems, out_sems,
):
    tokens, width = out_grad.shape
    pieces = width // LANES
    top = place.shape[0]
    peers = returned.shape[0]
    share = gain_grad.shape[1]
    body_rows = returned.shape[1] - EXTRA
    parts = sems.shape[0]
    step = peers // parts
    small = [
        pltpu.make_async_copy(source, target, in_sems.at[i])
        for i, (source, target) in enumerate(
            ((layer_in, x), (inverse_in, inverse), (place_in, place), (gain_in, gain_rows), (out_grad, grad))
        )
    ]
    for copy in small[:2]:
        copy.start()
    copies = []
    for i in range(parts):
        cut = pl.ds(i * step, step)
        copies.append(pltpu.make_async_copy(returned.at[cut], held.at[cut], sems.at[i]))
        copies[i].start()
    for copy in small[2:]:
        copy.start()
    for copy in small[:2]:
        copy.wait()

    def spread(group, carry):
        first = pl.multiple_of(group * GROUP, GROUP)
        scale = inverse[pl.ds(first, GROUP), :]
        for piece in range(pieces):
            units[strip(group, piece, pieces), :] = columns_of(x, first, piece) * scale
        return carry

    lax.fori_loop(0, tokens // GROUP, spread, 0)
    for copy in small[2:] + copies:
        copy.wait()

    def combine(block, carry):
        for i in range(4):
            token = block * 4 + i
            wheres = [place[k, token] for k in range(top)]
            total = jnp.zeros((pieces, LANES), F32)
            for where in wheres:
                total = total + held[where >> 3, slot_rows(where & 7, pieces), :].astype(F32)
            q = total * gain_rows[...]
            sums[token_rows(token, pieces), :] = q
            along = q * units[token_rows(token, pieces), :]
            dots[pl.ds(token, 1), :] = jnp.sum(along, axis=0, keepdims=True)
        return carry

    lax.fori_loop(0, tokens // 4, combine, 0)
    means = jnp.sum(dots[...], axis=-1, keepdims=True) / width
    dots[...] = inverse[...] * means

    def finish(group, carry):
        first = pl.multiple_of(group * GROUP, GROUP)
        scale = inverse[pl.ds(first, GROUP), :]
        lean = dots[pl.ds(first, GROUP), :]
        for piece in range(pieces):
            cut = slice(piece * LANES, (piece + 1) * LANES)
            q = sums[strip(group, piece, pieces), :]
            result[pl.ds(first, GROUP), cut] = (
                columns_of(grad, first, piece) + (q - columns_of(x, first, piece) * lean) * scale
            ).astype(BF16)
        return carry

    out_parts = out_sems.shape[0]
    part = tokens // out_parts
    sent = []
    for i in range(out_parts):
        lax.fori_loop(i * part // GROUP, (i + 1) * part // GROUP, finish, 0)
        cut = pl.ds(i * part, part)
        sent.append(pltpu.make_async_copy(result.at[cut], input_grad.at[cut], out_sems.at[i]))
        sent[i].start()

    def add_peers(block, total):
        for i in range(8):
            total = total + held[block * 8 + i, body_rows : body_rows + EXTRA, :].astype(F32)
        return total

    total = lax.fori_loop(0, peers // 8, add_peers, jnp.zeros((EXTRA, LANES), F32))[0:1]
    gain_grad[...] = (
        total[:, :share] + total[:, share : 2 * share] + total[:, 2 * share : 3 * share]
    )
    for copy in sent:
        copy.wait()


def transposed(left, right):
    return lax.dot_general(left, right, (((1,), (1,)), ((), ())), preferred_element_type=F32)


def exchange(buffer):
    return lax.all_to_all(buffer, ("dev", "role"), split_axis=0, concat_axis=0, tiled=True)


def three_parts(values):
    high = lax.reduce_precision(values, 8, 7)
    middle = lax.reduce_precision(values - high, 8, 7)
    low = values - high - middle
    return high.astype(BF16), middle.astype(BF16), low.astype(BF16)


def body(layer_in, norm_gain, routes, gate_weights, out_grad, expert_gate_up, expert_down):
    tokens, width = layer_in.shape
    top = routes.shape[1]
    peers = lax.axis_size(AXES)
    slots = tokens * top * 5 // (4 * peers)
    pieces = width // LANES
    chips = lax.axis_size("dev")
    hidden_units = expert_down.shape[1]
    row_count = peers * slots
    block = (peers, slots * pieces, LANES)
    gain = norm_gain.reshape(1, width)
    by_choice = routes.T
    weights = gate_weights.T
    token_scratch = pltpu.VMEM((tokens * pieces, LANES), F32)

    in_parts, out_parts = 4, 8
    send_rows, place, inverse = pl.pallas_call(
        functools.partial(send_rows_kernel, chips),
        out_shape=(
            jax.ShapeDtypeStruct(block, BF16),
            jax.ShapeDtypeStruct((top, tokens), jnp.int32),
            jax.ShapeDtypeStruct((tokens, LANES), F32),
        ),
        in_specs=[HBM, HBM, HBM],
        out_specs=(HBM, HBM, HBM),
        scratch_shapes=[
            pltpu.SMEM((top, tokens), jnp.int32),
            pltpu.VMEM((tokens, width), BF16),
            pltpu.VMEM((1, width), F32),
            pltpu.VMEM((tokens // in_parts * pieces, LANES), F32),
            pltpu.VMEM(((tokens + 1) * pieces, LANES), BF16),
            pltpu.VMEM(block, BF16),
            pltpu.VMEM((tokens, LANES), F32),
            pltpu.SMEM((top, tokens), jnp.int32),
            pltpu.SMEM((peers,), jnp.int32),
            pltpu.SMEM((peers * 8,), jnp.int32),
            pltpu.SemaphoreType.DMA((in_parts + 2,)),
            pltpu.SemaphoreType.DMA((out_parts + 2,)),
        ],
        compiler_params=WHOLE,
        name="send_rows",
    )(by_choice, layer_in, gain)
    arrived = exchange(send_rows).reshape(row_count, pieces, LANES).reshape(row_count, width)

    send_grads = pl.pallas_call(
        send_grads_kernel,
        out_shape=jax.ShapeDtypeStruct(block, BF16),
        in_specs=[SMEM, SMEM, VMEM],
        out_specs=VMEM,
        scratch_shapes=[token_scratch],
        compiler_params=PARAMS,
        name="send_grads",
    )(place, weights, out_grad)
    grad_rows = exchange(send_grads).reshape(row_count, pieces, LANES).reshape(row_count, width)

    w_gate_up = expert_gate_up[0]
    w_down = expert_down[0]
    projected = jnp.dot(arrived, w_gate_up, preferred_element_type=F32)
    g = projected[:, :hidden_units]
    u = projected[:, hidden_units:]
    s = jax.nn.sigmoid(g)
    active = g * s
    hidden = (active * u).astype(BF16)
    expert_rows = jnp.dot(hidden, w_down, preferred_element_type=F32).astype(BF16)
    returned = exchange(expert_rows.reshape(row_count, pieces, LANES).reshape(block))

    hidden_grad = transposed(grad_rows, w_down)
    gate_part = hidden_grad * u * s * (1.0 + g * (1.0 - s))
    pre_grad = jnp.concatenate([gate_part, hidden_grad * active], axis=-1).astype(BF16)
    back_rows = transposed(pre_grad, w_gate_up).astype(BF16)
    terms = jnp.sum(back_rows.astype(F32) * arrived.astype(F32), axis=0) / norm_gain
    share = width // peers
    parts = jnp.concatenate(
        [
            jnp.swapaxes(p.reshape(peers // chips, chips, share), 0, 1).reshape(peers, share)
            for p in three_parts(terms)
        ],
        axis=-1,
    )
    parts = jnp.pad(parts[:, None, :], ((0, 0), (0, EXTRA - 1), (0, LANES - 3 * share)))
    send_back = jnp.concatenate(
        [back_rows.reshape(row_count, pieces, LANES).reshape(block), parts], axis=1
    )
    came_back = exchange(send_back)

    layer_out, gate_grad = pl.pallas_call(
        outputs_kernel,
        out_shape=(
            jax.ShapeDtypeStruct((tokens, width), BF16),
            jax.ShapeDtypeStruct((top, tokens), F32),
        ),
        in_specs=[SMEM, SMEM, VMEM, VMEM, VMEM],
        out_specs=(VMEM, VMEM),
        scratch_shapes=[token_scratch, token_scratch, pltpu.VMEM((top, tokens, LANES), F32)],
        compiler_params=PARAMS,
        name="outputs",
    )(place, weights, layer_in, out_grad, returned)

    input_grad, gain_grad = pl.pallas_call(
        input_grad_kernel,
        out_shape=(
            jax.ShapeDtypeStruct((tokens, width), BF16),
            jax.ShapeDtypeStruct((1, share), F32),
        ),
        in_specs=[HBM] * 6,
        out_specs=(HBM, VMEM),
        scratch_shapes=[
            pltpu.SMEM((top, tokens), jnp.int32),
            pltpu.VMEM((tokens, width), BF16),
            pltpu.VMEM((tokens, LANES), F32),
            pltpu.VMEM((pieces, LANES), F32),
            pltpu.VMEM((tokens, width), BF16),
            pltpu.VMEM(came_back.shape, BF16),
            token_scratch,
            token_scratch,
            pltpu.VMEM((tokens, LANES), F32),
            pltpu.VMEM((tokens, width), BF16),
            pltpu.SemaphoreType.DMA((5,)),
            pltpu.SemaphoreType.DMA((8,)),
            pltpu.SemaphoreType.DMA((4,)),
        ],
        compiler_params=WHOLE,
        name="input_grad",
    )(place, layer_in, inverse, norm_gain.reshape(pieces, LANES), out_grad, came_back)
    gain_grad = gain_grad.reshape(share)
    return (layer_out, input_grad, gate_grad.T, gain_grad)


def solution(mesh):
    split = P(AXES, None)
    in_specs = (split, P(), split, split, split, P(AXES, None, None), P(AXES, None, None))
    out_specs = (split, split, split, P(AXES))
    return jax.shard_map(body, mesh=mesh, in_specs=in_specs, out_specs=out_specs, check_vma=False)
```

```python
import functools

import jax
import jax.numpy as jnp
from jax import lax
from jax.experimental import pallas as pl
from jax.experimental.pallas import tpu as pltpu
from jax.sharding import PartitionSpec as P

AXES = ("role", "dev")
EPSILON = 1e-06
LANES = 128
GROUP = 16
EXTRA = 8
F32 = jnp.float32
BF16 = jnp.bfloat16
VMEM = pl.BlockSpec(memory_space=pltpu.VMEM)
SMEM = pl.BlockSpec(memory_space=pltpu.SMEM)
HBM = pl.BlockSpec(memory_space=pltpu.HBM)
PARAMS = pltpu.CompilerParams(vmem_limit_bytes=40 * 1024 * 1024)
SMALL = pltpu.CompilerParams(vmem_limit_bytes=24 * 1024 * 1024)
WHOLE = pltpu.CompilerParams(vmem_limit_bytes=60 * 1024 * 1024)


def zero_fill(ref, step):
    def one(i, carry):
        rows = pl.ds(pl.multiple_of(i * step, step), step)
        ref[rows, :] = jnp.zeros((step, ref.shape[1]), ref.dtype)
        return carry

    lax.fori_loop(0, ref.shape[0] // step, one, 0)


def columns_of(ref, first, piece):
    return ref[pl.ds(first, GROUP), piece * LANES : (piece + 1) * LANES].astype(F32)


def strip(group, piece, pieces):
    return pl.ds(group * GROUP * pieces + piece, GROUP, stride=pieces)


def token_rows(token, pieces):
    return pl.ds(pl.multiple_of(token * pieces, pieces), pieces)


def slot_rows(where, pieces):
    return pl.ds(pl.multiple_of(where, pieces), pieces)


def send_rows_kernel(
    chip_count, routes_in, layer_in, gain, out, place_out, inverse_out,
    routes, x, gain_row, spread, packed, staged, inverses, place, count, table, in_sems, out_sems,
):
    tokens, width = layer_in.shape
    pieces = width // LANES
    top = routes.shape[0]
    peers = out.shape[0]
    slots = out.shape[1] // pieces
    cores = peers // chip_count
    shift = pieces.bit_length() - 1
    in_parts, out_parts = in_sems.shape[0] - 2, out_sems.shape[0] - 2
    part = tokens // in_parts
    copies = []
    for i in range(in_parts):
        cut = pl.ds(i * part, part)
        copies.append(pltpu.make_async_copy(layer_in.at[cut], x.at[cut], in_sems.at[i]))
    gain_copy = pltpu.make_async_copy(gain, gain_row, in_sems.at[in_parts])
    routes_copy = pltpu.make_async_copy(routes_in, routes, in_sems.at[in_parts + 1])
    copies[0].start()
    gain_copy.start()
    routes_copy.start()
    for copy in copies[1:]:
        copy.start()

    def clear(chip, carry):
        for core in range(cores):
            peer = chip * cores + core
            count[core * chip_count + chip] = peer * (slots * pieces)
            for slot in range(slots):
                table[peer * slots + slot] = tokens
        return carry

    lax.fori_loop(0, chip_count, clear, 0)
    packed[pl.ds(tokens * pieces, pieces), :] = jnp.zeros((pieces, LANES), BF16)
    routes_copy.wait()
    gain_copy.wait()

    def take_part(first):
        groups = range(first, first + part, GROUP)
        for at in groups:
            square = jnp.zeros((GROUP, LANES), F32)
            for piece in range(pieces):
                values = columns_of(x, at, piece)
                square = square + values * values
            root_mean = jnp.sqrt(jnp.sum(square, axis=-1, keepdims=True) / width + EPSILON)
            inverses[pl.ds(at, GROUP), :] = jnp.broadcast_to(1.0 / root_mean, (GROUP, LANES))
        for at in groups:
            inverse = inverses[pl.ds(at, GROUP), :]
            for piece in range(pieces):
                unit = columns_of(x, at, piece) * inverse
                spread[pl.ds((at - first) * pieces + piece, GROUP, stride=pieces), :] = (
                    unit * gain_row[:, piece * LANES : (piece + 1) * LANES]
                )
        packed[first * pieces : (first + part) * pieces, :] = spread[...].astype(BF16)
        for token in range(first, first + part):
            experts = [routes[k, token] for k in range(top)]
            wheres = [count[expert] for expert in experts]
            for k in range(top):
                count[experts[k]] = wheres[k] + pieces
                place[k, token] = wheres[k]
                table[wheres[k] >> shift] = token

    for i in range(in_parts):
        copies[i].wait()
        take_part(i * part)
    sent = [
        pltpu.make_async_copy(place, place_out, out_sems.at[out_parts]),
        pltpu.make_async_copy(inverses, inverse_out, out_sems.at[out_parts + 1]),
    ]
    for copy in sent:
        copy.start()
    step = peers // out_parts

    def fill(pair, carry):
        for i in range(2):
            peer = pair * 2 + i
            chosen = [table[peer * slots + slot] for slot in range(slots)]
            for slot in range(slots):
                staged[peer, slot * pieces : (slot + 1) * pieces, :] = packed[
                    token_rows(chosen[slot], pieces), :
                ]
        return carry

    for i in range(out_parts):
        lax.fori_loop(i * step // 2, (i + 1) * step // 2, fill, 0)
        cut = pl.ds(i * step, step)
        sent.append(pltpu.make_async_copy(staged.at[cut], out.at[cut], out_sems.at[i]))
        sent[-1].start()
    for copy in sent:
        copy.wait()


def send_grads_kernel(place, weights, out_grad, out, rows):
    tokens, width = out_grad.shape
    pieces = width // LANES
    top = place.shape[0]
    zero_fill(out, pieces * top)

    def spread(group, carry):
        first = pl.multiple_of(group * GROUP, GROUP)
        for piece in range(pieces):
            rows[strip(group, piece, pieces), :] = columns_of(out_grad, first, piece)
        return carry

    lax.fori_loop(0, tokens // GROUP, spread, 0)

    def place_token(token, carry):
        row = rows[token_rows(token, pieces), :]
        for k in range(top):
            out[slot_rows(place[k, token], pieces), :] = (row * weights[k, token]).astype(BF16)
        return carry

    lax.fori_loop(0, tokens, place_token, 0)


def outputs_kernel(place, weights, layer_in, out_grad, returned, layer_out, gate_grad, rows, sums, dots):
    tokens, width = out_grad.shape
    pieces = width // LANES
    top = place.shape[0]

    def spread(group, carry):
        first = pl.multiple_of(group * GROUP, GROUP)
        for piece in range(pieces):
            rows[strip(group, piece, pieces), :] = columns_of(out_grad, first, piece)
        return carry

    lax.fori_loop(0, tokens // GROUP, spread, 0)

    def combine(token, carry):
        grad = rows[token_rows(token, pieces), :]
        total = jnp.zeros((pieces, LANES), F32)
        for k in range(top):
            row = returned[slot_rows(place[k, token], pieces), :].astype(F32)
            total = total + weights[k, token] * row
            dots[k, pl.ds(token, 1), :] = jnp.sum(row * grad, axis=0, keepdims=True)
        sums[token_rows(token, pieces), :] = total
        return carry

    lax.fori_loop(0, tokens, combine, 0)
    for k in range(top):
        gate_grad[k : k + 1, :] = jnp.sum(dots[k].T, axis=0, keepdims=True)

    def finish(group, carry):
        first = pl.multiple_of(group * GROUP, GROUP)
        for piece in range(pieces):
            x = columns_of(layer_in, first, piece)
            layer_out[pl.ds(first, GROUP), piece * LANES : (piece + 1) * LANES] = (
                x + sums[strip(group, piece, pieces), :]
            ).astype(BF16)
        return carry

    lax.fori_loop(0, tokens // GROUP, finish, 0)


def input_grad_kernel(
    place_in, x, inverse, gain_rows, grad, returned, input_grad, gain_grad,
    place, held, extra, units, sums, dots, result, place_sem, sems, extra_sem, out_sems,
):
    tokens, width = grad.shape
    pieces = width // LANES
    top = place.shape[0]
    peers = returned.shape[0]
    share = gain_grad.shape[1]
    body_rows = returned.shape[1] - EXTRA
    parts = sems.shape[0]
    step = peers // parts
    blocks = held.reshape(peers, body_rows, LANES)
    copies = []
    for i in range(parts):
        cut = pl.ds(i * step, step)
        copies.append(
            pltpu.make_async_copy(returned.at[cut, pl.ds(0, body_rows)], blocks.at[cut], sems.at[i])
        )
    copies.append(pltpu.make_async_copy(place_in, place, place_sem))
    copies.append(
        pltpu.make_async_copy(returned.at[:, pl.ds(body_rows, EXTRA)], extra, extra_sem)
    )
    for copy in copies:
        copy.start()

    def spread(group, carry):
        first = pl.multiple_of(group * GROUP, GROUP)
        scale = inverse[pl.ds(first, GROUP), :]
        for piece in range(pieces):
            units[strip(group, piece, pieces), :] = columns_of(x, first, piece) * scale
        return carry

    lax.fori_loop(0, tokens // GROUP, spread, 0)
    for copy in copies:
        copy.wait()

    def combine(block, carry):
        for i in range(4):
            token = block * 4 + i
            wheres = [place[k, token] for k in range(top)]
            total = jnp.zeros((pieces, LANES), F32)
            for where in wheres:
                total = total + held[slot_rows(where, pieces), :].astype(F32)
            q = total * gain_rows[...]
            sums[token_rows(token, pieces), :] = q
            along = q * units[token_rows(token, pieces), :]
            dots[pl.ds(token, 1), :] = jnp.sum(along, axis=0, keepdims=True)
        return carry

    lax.fori_loop(0, tokens // 4, combine, 0)
    dots[...] = inverse[...] * (jnp.sum(dots[...], axis=-1, keepdims=True) / width)

    def finish(group, carry):
        first = pl.multiple_of(group * GROUP, GROUP)
        scale = inverse[pl.ds(first, GROUP), :]
        lean = dots[pl.ds(first, GROUP), :]
        for piece in range(pieces):
            cut = slice(piece * LANES, (piece + 1) * LANES)
            q = sums[strip(group, piece, pieces), :]
            result[pl.ds(first, GROUP), cut] = (
                columns_of(grad, first, piece) + (q - columns_of(x, first, piece) * lean) * scale
            ).astype(BF16)
        return carry

    def add_peers(block, total):
        for i in range(8):
            total = total + extra[block * 8 + i].astype(F32)
        return total

    out_parts = out_sems.shape[0]
    part = tokens // out_parts
    sent = []
    for i in range(out_parts):
        lax.fori_loop(i * part // GROUP, (i + 1) * part // GROUP, finish, 0)
        cut = pl.ds(i * part, part)
        sent.append(pltpu.make_async_copy(result.at[cut], input_grad.at[cut], out_sems.at[i]))
        sent[i].start()
    total = lax.fori_loop(0, peers // 8, add_peers, jnp.zeros((EXTRA, LANES), F32))[0:1]
    gain_grad[...] = (
        total[:, :share] + total[:, share : 2 * share] + total[:, 2 * share : 3 * share]
    )
    for copy in sent:
        copy.wait()


def transposed(left, right):
    return lax.dot_general(left, right, (((1,), (1,)), ((), ())), preferred_element_type=F32)


def exchange(buffer):
    return lax.all_to_all(buffer, ("dev", "role"), split_axis=0, concat_axis=0, tiled=True)


def three_parts(values):
    high = lax.reduce_precision(values, 8, 7)
    middle = lax.reduce_precision(values - high, 8, 7)
    low = values - high - middle
    return high.astype(BF16), middle.astype(BF16), low.astype(BF16)


def body(layer_in, norm_gain, routes, gate_weights, out_grad, expert_gate_up, expert_down):
    tokens, width = layer_in.shape
    top = routes.shape[1]
    peers = lax.axis_size(AXES)
    slots = tokens * top * 5 // (4 * peers)
    pieces = width // LANES
    chips = lax.axis_size("dev")
    hidden_units = expert_down.shape[1]
    row_count = peers * slots
    block = (peers, slots * pieces, LANES)
    gain = norm_gain.reshape(1, width)
    by_choice = routes.T
    weights = gate_weights.T
    token_scratch = pltpu.VMEM((tokens * pieces, LANES), F32)

    in_parts, out_parts = 4, 8
    send_rows, place, inverse = pl.pallas_call(
        functools.partial(send_rows_kernel, chips),
        out_shape=(
            jax.ShapeDtypeStruct(block, BF16),
            jax.ShapeDtypeStruct((top, tokens), jnp.int32),
            jax.ShapeDtypeStruct((tokens, LANES), F32),
        ),
        in_specs=[HBM, HBM, HBM],
        out_specs=(HBM, HBM, HBM),
        scratch_shapes=[
            pltpu.SMEM((top, tokens), jnp.int32),
            pltpu.VMEM((tokens, width), BF16),
            pltpu.VMEM((1, width), F32),
            pltpu.VMEM((tokens // in_parts * pieces, LANES), F32),
            pltpu.VMEM(((tokens + 1) * pieces, LANES), BF16),
            pltpu.VMEM(block, BF16),
            pltpu.VMEM((tokens, LANES), F32),
            pltpu.SMEM((top, tokens), jnp.int32),
            pltpu.SMEM((peers,), jnp.int32),
            pltpu.SMEM((row_count,), jnp.int32),
            pltpu.SemaphoreType.DMA((in_parts + 2,)),
            pltpu.SemaphoreType.DMA((out_parts + 2,)),
        ],
        compiler_params=WHOLE,
        name="send_rows",
    )(by_choice, layer_in, gain)
    arrived = exchange(send_rows).reshape(row_count, pieces, LANES).reshape(row_count, width)

    send_grads = pl.pallas_call(
        send_grads_kernel,
        out_shape=jax.ShapeDtypeStruct((row_count * pieces, LANES), BF16),
        in_specs=[SMEM, SMEM, VMEM],
        out_specs=VMEM,
        scratch_shapes=[token_scratch],
        compiler_params=PARAMS,
        name="send_grads",
    )(place, weights, out_grad)
    grad_rows = exchange(send_grads.reshape(block)).reshape(row_count, pieces, LANES).reshape(row_count, width)

    w_gate_up = expert_gate_up[0]
    w_down = expert_down[0]
    projected = jnp.dot(arrived, w_gate_up, preferred_element_type=F32)
    g = projected[:, :hidden_units]
    u = projected[:, hidden_units:]
    s = jax.nn.sigmoid(g)
    active = g * s
    hidden = (active * u).astype(BF16)
    expert_rows = jnp.dot(hidden, w_down, preferred_element_type=F32).astype(BF16)
    returned = exchange(expert_rows.reshape(row_count, pieces, LANES).reshape(block))

    hidden_grad = transposed(grad_rows, w_down)
    gate_part = hidden_grad * u * s * (1.0 + g * (1.0 - s))
    pre_grad = jnp.concatenate([gate_part, hidden_grad * active], axis=-1).astype(BF16)
    back_rows = transposed(pre_grad, w_gate_up).astype(BF16)
    terms = jnp.sum(back_rows.astype(F32) * arrived.astype(F32), axis=0) / norm_gain
    share = width // peers
    parts = jnp.concatenate(
        [
            jnp.swapaxes(p.reshape(peers // chips, chips, share), 0, 1).reshape(peers, share)
            for p in three_parts(terms)
        ],
        axis=-1,
    )
    parts = jnp.pad(parts[:, None, :], ((0, 0), (0, EXTRA - 1), (0, LANES - 3 * share)))
    send_back = jnp.concatenate(
        [back_rows.reshape(row_count, pieces, LANES).reshape(block), parts], axis=1
    )
    came_back = exchange(send_back)

    layer_out, gate_grad = pl.pallas_call(
        outputs_kernel,
        out_shape=(
            jax.ShapeDtypeStruct((tokens, width), BF16),
            jax.ShapeDtypeStruct((top, tokens), F32),
        ),
        in_specs=[SMEM, SMEM, VMEM, VMEM, VMEM],
        out_specs=(VMEM, VMEM),
        scratch_shapes=[token_scratch, token_scratch, pltpu.VMEM((top, tokens, LANES), F32)],
        compiler_params=SMALL,
        name="outputs",
    )(place, weights, layer_in, out_grad, returned.reshape(row_count * pieces, LANES))

    input_grad, gain_grad = pl.pallas_call(
        input_grad_kernel,
        out_shape=(
            jax.ShapeDtypeStruct((tokens, width), BF16),
            jax.ShapeDtypeStruct((1, share), F32),
        ),
        in_specs=[HBM, VMEM, VMEM, VMEM, VMEM, HBM],
        out_specs=(HBM, VMEM),
        scratch_shapes=[
            pltpu.SMEM((top, tokens), jnp.int32),
            pltpu.VMEM((row_count * pieces, LANES), BF16),
            pltpu.VMEM((peers, EXTRA, LANES), BF16),
            token_scratch,
            token_scratch,
            pltpu.VMEM((tokens, LANES), F32),
            pltpu.VMEM((tokens, width), BF16),
            pltpu.SemaphoreType.DMA(()),
            pltpu.SemaphoreType.DMA((8,)),
            pltpu.SemaphoreType.DMA(()),
            pltpu.SemaphoreType.DMA((8,)),
        ],
        compiler_params=SMALL,
        name="input_grad",
    )(place, layer_in, inverse, norm_gain.reshape(pieces, LANES), out_grad, came_back)
    gain_grad = gain_grad.reshape(share)
    return (layer_out, input_grad, gate_grad.T, gain_grad)


def solution(mesh):
    split = P(AXES, None)
    in_specs = (split, P(), split, split, split, P(AXES, None, None), P(AXES, None, None))
    out_specs = (split, split, split, P(AXES))
    return jax.shard_map(body, mesh=mesh, in_specs=in_specs, out_specs=out_specs, check_vma=False)
```

```python
import functools

import jax
import jax.numpy as jnp
from jax import lax
from jax.experimental import pallas as pl
from jax.experimental.pallas import tpu as pltpu
from jax.sharding import PartitionSpec as P

AXES = ("role", "dev")
EPSILON = 1e-06
LANES = 128
GROUP = 16
PAIR = 2
F32 = jnp.float32
BF16 = jnp.bfloat16
VMEM = pl.BlockSpec(memory_space=pltpu.VMEM)
SMEM = pl.BlockSpec(memory_space=pltpu.SMEM)
HBM = pl.BlockSpec(memory_space=pltpu.HBM)
PARAMS = pltpu.CompilerParams(vmem_limit_bytes=40 * 1024 * 1024)
SMALL = pltpu.CompilerParams(vmem_limit_bytes=24 * 1024 * 1024)
WHOLE = pltpu.CompilerParams(vmem_limit_bytes=60 * 1024 * 1024)


def zero_fill(ref, step):
    def one(i, carry):
        rows = pl.ds(pl.multiple_of(i * step, step), step)
        ref[rows, :] = jnp.zeros((step, ref.shape[1]), ref.dtype)
        return carry

    lax.fori_loop(0, ref.shape[0] // step, one, 0)


def columns_of(ref, first, piece):
    return ref[pl.ds(first, GROUP), piece * LANES : (piece + 1) * LANES].astype(F32)


def strip(group, piece, pieces):
    return pl.ds(group * GROUP * pieces + piece, GROUP, stride=pieces)


def token_rows(token, pieces):
    return pl.ds(pl.multiple_of(token * pieces, pieces), pieces)


def slot_rows(where, pieces):
    return pl.ds(pl.multiple_of(where, pieces), pieces)


def send_rows_kernel(
    chip_count, routes_in, layer_in, gain, out, place_out, inverse_out,
    routes, x, gain_row, spread, packed, staged, inverses, place, count, table, in_sems, out_sems,
):
    tokens, width = layer_in.shape
    pieces = width // LANES
    top = routes.shape[0]
    peers = out.shape[0]
    slots = out.shape[1] // pieces
    cores = peers // chip_count
    shift = pieces.bit_length() - 1
    in_parts, out_parts = in_sems.shape[0] - 2, out_sems.shape[0] - 2
    part = tokens // in_parts
    copies = []
    for i in range(in_parts):
        cut = pl.ds(i * part, part)
        copies.append(pltpu.make_async_copy(layer_in.at[cut], x.at[cut], in_sems.at[i]))
    gain_copy = pltpu.make_async_copy(gain, gain_row, in_sems.at[in_parts])
    routes_copy = pltpu.make_async_copy(routes_in, routes, in_sems.at[in_parts + 1])
    copies[0].start()
    gain_copy.start()
    routes_copy.start()
    for copy in copies[1:]:
        copy.start()

    def clear(chip, carry):
        for core in range(cores):
            peer = chip * cores + core
            count[core * chip_count + chip] = peer * (slots * pieces)
            for slot in range(slots):
                table[peer * slots + slot] = tokens
        return carry

    lax.fori_loop(0, chip_count, clear, 0)
    packed[pl.ds(tokens * pieces, pieces), :] = jnp.zeros((pieces, LANES), BF16)
    routes_copy.wait()
    gain_copy.wait()

    def take_part(first):
        groups = range(first, first + part, GROUP)
        for at in groups:
            square = jnp.zeros((GROUP, LANES), F32)
            for piece in range(pieces):
                values = columns_of(x, at, piece)
                square = square + values * values
            root_mean = jnp.sqrt(jnp.sum(square, axis=-1, keepdims=True) / width + EPSILON)
            inverses[pl.ds(at, GROUP), :] = jnp.broadcast_to(1.0 / root_mean, (GROUP, LANES))
        for at in groups:
            inverse = inverses[pl.ds(at, GROUP), :]
            for piece in range(pieces):
                unit = columns_of(x, at, piece) * inverse
                spread[pl.ds((at - first) * pieces + piece, GROUP, stride=pieces), :] = (
                    unit * gain_row[:, piece * LANES : (piece + 1) * LANES]
                )
        packed[first * pieces : (first + part) * pieces, :] = spread[...].astype(BF16)
        for token in range(first, first + part):
            experts = [routes[k, token] for k in range(top)]
            wheres = [count[expert] for expert in experts]
            for k in range(top):
                count[experts[k]] = wheres[k] + pieces
                place[k, token] = wheres[k]
                table[wheres[k] >> shift] = token

    for i in range(in_parts):
        copies[i].wait()
        take_part(i * part)
    sent = [
        pltpu.make_async_copy(place, place_out, out_sems.at[out_parts]),
        pltpu.make_async_copy(inverses, inverse_out, out_sems.at[out_parts + 1]),
    ]
    for copy in sent:
        copy.start()
    step = peers // out_parts

    def fill(pair, carry):
        for i in range(2):
            peer = pair * 2 + i
            chosen = [table[peer * slots + slot] for slot in range(slots)]
            for slot in range(slots):
                staged[peer, slot * pieces : (slot + 1) * pieces, :] = packed[
                    token_rows(chosen[slot], pieces), :
                ]
        return carry

    for i in range(out_parts):
        lax.fori_loop(i * step // 2, (i + 1) * step // 2, fill, 0)
        cut = pl.ds(i * step, step)
        sent.append(pltpu.make_async_copy(staged.at[cut], out.at[cut], out_sems.at[i]))
        sent[-1].start()
    for copy in sent:
        copy.wait()


def send_grads_kernel(place, weights, out_grad, out, rows):
    tokens, width = out_grad.shape
    pieces = width // LANES
    top = place.shape[0]
    zero_fill(out, pieces * top)

    def spread(group, carry):
        first = pl.multiple_of(group * GROUP, GROUP)
        for piece in range(pieces):
            rows[strip(group, piece, pieces), :] = columns_of(out_grad, first, piece)
        return carry

    lax.fori_loop(0, tokens // GROUP, spread, 0)

    def place_token(token, carry):
        row = rows[token_rows(token, pieces), :]
        for k in range(top):
            out[slot_rows(place[k, token], pieces), :] = (row * weights[k, token]).astype(BF16)
        return carry

    lax.fori_loop(0, tokens, place_token, 0)


def outputs_kernel(place, weights, layer_in, out_grad, returned, layer_out, gate_grad, rows, sums, dots):
    tokens, width = out_grad.shape
    pieces = width // LANES
    top = place.shape[0]

    def spread(group, carry):
        first = pl.multiple_of(group * GROUP, GROUP)
        for piece in range(pieces):
            rows[strip(group, piece, pieces), :] = columns_of(out_grad, first, piece)
        return carry

    lax.fori_loop(0, tokens // GROUP, spread, 0)

    def combine(token, carry):
        grad = rows[token_rows(token, pieces), :]
        total = jnp.zeros((pieces, LANES), F32)
        for k in range(top):
            row = returned[slot_rows(place[k, token], pieces), :].astype(F32)
            total = total + weights[k, token] * row
            dots[k, pl.ds(token, 1), :] = jnp.sum(row * grad, axis=0, keepdims=True)
        sums[token_rows(token, pieces), :] = total
        return carry

    lax.fori_loop(0, tokens, combine, 0)
    for k in range(top):
        gate_grad[k : k + 1, :] = jnp.sum(dots[k].T, axis=0, keepdims=True)

    def finish(group, carry):
        first = pl.multiple_of(group * GROUP, GROUP)
        for piece in range(pieces):
            x = columns_of(layer_in, first, piece)
            layer_out[pl.ds(first, GROUP), piece * LANES : (piece + 1) * LANES] = (
                x + sums[strip(group, piece, pieces), :]
            ).astype(BF16)
        return carry

    lax.fori_loop(0, tokens // GROUP, finish, 0)


def input_grad_kernel(
    place_in, x, inverse, gain_rows, grad, returned, input_grad, gain_grad,
    place, held, extra, units, sums, dots, result, place_sem, sems, extra_sem, out_sems,
):
    tokens, width = grad.shape
    pieces = width // LANES
    top = place.shape[0]
    peers, pairs = returned.shape[:2]
    share = gain_grad.shape[1]
    body_rows = (pairs - 1) * PAIR
    arrived = returned.reshape(peers, pairs * PAIR, LANES)
    parts = sems.shape[0]
    step = peers // parts
    blocks = held.reshape(peers, body_rows, LANES)
    copies = []
    for i in range(parts):
        cut = pl.ds(i * step, step)
        copies.append(
            pltpu.make_async_copy(arrived.at[cut, pl.ds(0, body_rows)], blocks.at[cut], sems.at[i])
        )
    copies.append(pltpu.make_async_copy(place_in, place, place_sem))
    copies.append(pltpu.make_async_copy(returned.at[:, pl.ds(pairs - 1, 1)], extra, extra_sem))
    for copy in copies:
        copy.start()

    def spread(group, carry):
        first = pl.multiple_of(group * GROUP, GROUP)
        scale = inverse[pl.ds(first, GROUP), :]
        for piece in range(pieces):
            units[strip(group, piece, pieces), :] = columns_of(x, first, piece) * scale
        return carry

    lax.fori_loop(0, tokens // GROUP, spread, 0)
    for copy in copies:
        copy.wait()

    def combine(block, carry):
        for i in range(4):
            token = block * 4 + i
            wheres = [place[k, token] for k in range(top)]
            total = jnp.zeros((pieces, LANES), F32)
            for where in wheres:
                total = total + held[slot_rows(where, pieces), :].astype(F32)
            q = total * gain_rows[...]
            sums[token_rows(token, pieces), :] = q
            along = q * units[token_rows(token, pieces), :]
            dots[pl.ds(token, 1), :] = jnp.sum(along, axis=0, keepdims=True)
        return carry

    lax.fori_loop(0, tokens // 4, combine, 0)
    dots[...] = inverse[...] * (jnp.sum(dots[...], axis=-1, keepdims=True) / width)

    def finish(group, carry):
        first = pl.multiple_of(group * GROUP, GROUP)
        scale = inverse[pl.ds(first, GROUP), :]
        lean = dots[pl.ds(first, GROUP), :]
        for piece in range(pieces):
            cut = slice(piece * LANES, (piece + 1) * LANES)
            q = sums[strip(group, piece, pieces), :]
            result[pl.ds(first, GROUP), cut] = (
                columns_of(grad, first, piece) + (q - columns_of(x, first, piece) * lean) * scale
            ).astype(BF16)
        return carry

    def add_peers(block, total):
        for i in range(8):
            total = total + extra[block * 8 + i, 0].astype(F32)
        return total

    out_parts = out_sems.shape[0]
    part = tokens // out_parts
    sent = []
    for i in range(out_parts):
        lax.fori_loop(i * part // GROUP, (i + 1) * part // GROUP, finish, 0)
        cut = pl.ds(i * part, part)
        sent.append(pltpu.make_async_copy(result.at[cut], input_grad.at[cut], out_sems.at[i]))
        sent[i].start()
    total = lax.fori_loop(0, peers // 8, add_peers, jnp.zeros((PAIR, LANES), F32))[0:1]
    gain_grad[...] = (
        total[:, :share] + total[:, share : 2 * share] + total[:, 2 * share : 3 * share]
    )
    for copy in sent:
        copy.wait()


def transposed(left, right):
    return lax.dot_general(left, right, (((1,), (1,)), ((), ())), preferred_element_type=F32)


def exchange(buffer):
    return lax.all_to_all(buffer, ("dev", "role"), split_axis=0, concat_axis=0, tiled=True)


def three_parts(values):
    high = lax.reduce_precision(values, 8, 7)
    middle = lax.reduce_precision(values - high, 8, 7)
    low = values - high - middle
    return high.astype(BF16), middle.astype(BF16), low.astype(BF16)


def body(layer_in, norm_gain, routes, gate_weights, out_grad, expert_gate_up, expert_down):
    tokens, width = layer_in.shape
    top = routes.shape[1]
    peers = lax.axis_size(AXES)
    slots = tokens * top * 5 // (4 * peers)
    pieces = width // LANES
    chips = lax.axis_size("dev")
    hidden_units = expert_down.shape[1]
    row_count = peers * slots
    block = (peers, slots * pieces, LANES)
    gain = norm_gain.reshape(1, width)
    by_choice = routes.T
    weights = gate_weights.T
    token_scratch = pltpu.VMEM((tokens * pieces, LANES), F32)

    in_parts, out_parts = 4, 8
    send_rows, place, inverse = pl.pallas_call(
        functools.partial(send_rows_kernel, chips),
        out_shape=(
            jax.ShapeDtypeStruct(block, BF16),
            jax.ShapeDtypeStruct((top, tokens), jnp.int32),
            jax.ShapeDtypeStruct((tokens, LANES), F32),
        ),
        in_specs=[HBM, HBM, HBM],
        out_specs=(HBM, HBM, HBM),
        scratch_shapes=[
            pltpu.SMEM((top, tokens), jnp.int32),
            pltpu.VMEM((tokens, width), BF16),
            pltpu.VMEM((1, width), F32),
            pltpu.VMEM((tokens // in_parts * pieces, LANES), F32),
            pltpu.VMEM(((tokens + 1) * pieces, LANES), BF16),
            pltpu.VMEM(block, BF16),
            pltpu.VMEM((tokens, LANES), F32),
            pltpu.SMEM((top, tokens), jnp.int32),
            pltpu.SMEM((peers,), jnp.int32),
            pltpu.SMEM((row_count,), jnp.int32),
            pltpu.SemaphoreType.DMA((in_parts + 2,)),
            pltpu.SemaphoreType.DMA((out_parts + 2,)),
        ],
        compiler_params=WHOLE,
        name="send_rows",
    )(by_choice, layer_in, gain)
    arrived = exchange(send_rows).reshape(row_count, pieces, LANES).reshape(row_count, width)

    send_grads = pl.pallas_call(
        send_grads_kernel,
        out_shape=jax.ShapeDtypeStruct((row_count * pieces, LANES), BF16),
        in_specs=[SMEM, SMEM, VMEM],
        out_specs=VMEM,
        scratch_shapes=[token_scratch],
        compiler_params=PARAMS,
        name="send_grads",
    )(place, weights, out_grad)
    grad_rows = exchange(send_grads.reshape(block)).reshape(row_count, pieces, LANES).reshape(row_count, width)

    w_gate_up = expert_gate_up[0]
    w_down = expert_down[0]
    projected = jnp.dot(arrived, w_gate_up, preferred_element_type=F32)
    g = projected[:, :hidden_units]
    u = projected[:, hidden_units:]
    s = jax.nn.sigmoid(g)
    active = g * s
    hidden = (active * u).astype(BF16)
    expert_rows = jnp.dot(hidden, w_down, preferred_element_type=F32).astype(BF16)
    returned = exchange(expert_rows.reshape(row_count, pieces, LANES).reshape(block))

    hidden_grad = transposed(grad_rows, w_down)
    gate_part = hidden_grad * u * s * (1.0 + g * (1.0 - s))
    pre_grad = jnp.concatenate([gate_part, hidden_grad * active], axis=-1).astype(BF16)
    back_rows = transposed(pre_grad, w_gate_up).astype(BF16)
    terms = jnp.sum(back_rows.astype(F32) * arrived.astype(F32), axis=0) / norm_gain
    share = width // peers
    parts = jnp.concatenate(
        [
            jnp.swapaxes(p.reshape(peers // chips, chips, share), 0, 1).reshape(peers, share)
            for p in three_parts(terms)
        ],
        axis=-1,
    )
    parts = jnp.pad(parts[:, None, None, :], ((0, 0), (0, 0), (0, PAIR - 1), (0, LANES - 3 * share)))
    back_pairs = back_rows.reshape(row_count, pieces, LANES).reshape(peers, -1, PAIR, LANES)
    send_back = jnp.concatenate([back_pairs, parts], axis=1)
    came_back = exchange(send_back)

    layer_out, gate_grad = pl.pallas_call(
        outputs_kernel,
        out_shape=(
            jax.ShapeDtypeStruct((tokens, width), BF16),
            jax.ShapeDtypeStruct((top, tokens), F32),
        ),
        in_specs=[SMEM, SMEM, VMEM, VMEM, VMEM],
        out_specs=(VMEM, VMEM),
        scratch_shapes=[token_scratch, token_scratch, pltpu.VMEM((top, tokens, LANES), F32)],
        compiler_params=SMALL,
        name="outputs",
    )(place, weights, layer_in, out_grad, returned.reshape(row_count * pieces, LANES))

    input_grad, gain_grad = pl.pallas_call(
        input_grad_kernel,
        out_shape=(
            jax.ShapeDtypeStruct((tokens, width), BF16),
            jax.ShapeDtypeStruct((1, share), F32),
        ),
        in_specs=[HBM, VMEM, VMEM, VMEM, VMEM, HBM],
        out_specs=(HBM, VMEM),
        scratch_shapes=[
            pltpu.SMEM((top, tokens), jnp.int32),
            pltpu.VMEM((row_count * pieces, LANES), BF16),
            pltpu.VMEM((peers, 1, PAIR, LANES), BF16),
            token_scratch,
            token_scratch,
            pltpu.VMEM((tokens, LANES), F32),
            pltpu.VMEM((tokens, width), BF16),
            pltpu.SemaphoreType.DMA(()),
            pltpu.SemaphoreType.DMA((8,)),
            pltpu.SemaphoreType.DMA(()),
            pltpu.SemaphoreType.DMA((8,)),
        ],
        compiler_params=SMALL,
        name="input_grad",
    )(place, layer_in, inverse, norm_gain.reshape(pieces, LANES), out_grad, came_back)
    gain_grad = gain_grad.reshape(share)
    return (layer_out, input_grad, gate_grad.T, gain_grad)


def solution(mesh):
    split = P(AXES, None)
    in_specs = (split, P(), split, split, split, P(AXES, None, None), P(AXES, None, None))
    out_specs = (split, split, split, P(AXES))
    return jax.shard_map(body, mesh=mesh, in_specs=in_specs, out_specs=out_specs, check_vma=False)
```

```python
import functools

import jax
import jax.numpy as jnp
from jax import lax
from jax.experimental import pallas as pl
from jax.experimental.pallas import tpu as pltpu
from jax.sharding import PartitionSpec as P

AXES = ("role", "dev")
EPSILON = 1e-06
LANES = 128
GROUP = 16
PAIR = 2
F32 = jnp.float32
BF16 = jnp.bfloat16
VMEM = pl.BlockSpec(memory_space=pltpu.VMEM)
SMEM = pl.BlockSpec(memory_space=pltpu.SMEM)
HBM = pl.BlockSpec(memory_space=pltpu.HBM)
PARAMS = pltpu.CompilerParams(vmem_limit_bytes=40 * 1024 * 1024)
SMALL = pltpu.CompilerParams(vmem_limit_bytes=24 * 1024 * 1024)
WHOLE = pltpu.CompilerParams(vmem_limit_bytes=60 * 1024 * 1024)


def zero_fill(ref, step):
    def one(i, carry):
        rows = pl.ds(pl.multiple_of(i * step, step), step)
        ref[rows, :] = jnp.zeros((step, ref.shape[1]), ref.dtype)
        return carry

    lax.fori_loop(0, ref.shape[0] // step, one, 0)


def columns_of(ref, first, piece):
    return ref[pl.ds(first, GROUP), piece * LANES : (piece + 1) * LANES].astype(F32)


def strip(group, piece, pieces):
    return pl.ds(group * GROUP * pieces + piece, GROUP, stride=pieces)


def token_rows(token, pieces):
    return pl.ds(pl.multiple_of(token * pieces, pieces), pieces)


def slot_rows(where, pieces):
    return pl.ds(pl.multiple_of(where, pieces), pieces)


def send_rows_kernel(
    chip_count, routes_in, layer_in, gain, out, place_out, inverse_out,
    routes, x, gain_row, spread, packed, staged, inverses, place, count, table, in_sems, out_sems,
):
    tokens, width = layer_in.shape
    pieces = width // LANES
    top = routes.shape[0]
    peers = out.shape[0]
    slots = out.shape[1] // pieces
    cores = peers // chip_count
    shift = pieces.bit_length() - 1
    in_parts, out_parts = in_sems.shape[0] - 2, out_sems.shape[0] - 2
    part = tokens // in_parts
    copies = []
    for i in range(in_parts):
        cut = pl.ds(i * part, part)
        copies.append(pltpu.make_async_copy(layer_in.at[cut], x.at[cut], in_sems.at[i]))
    gain_copy = pltpu.make_async_copy(gain, gain_row, in_sems.at[in_parts])
    routes_copy = pltpu.make_async_copy(routes_in, routes, in_sems.at[in_parts + 1])
    copies[0].start()
    gain_copy.start()
    routes_copy.start()
    for copy in copies[1:]:
        copy.start()

    def clear(chip, carry):
        for core in range(cores):
            peer = chip * cores + core
            count[core * chip_count + chip] = peer * (slots * pieces)
            for slot in range(slots):
                table[peer * slots + slot] = tokens
        return carry

    lax.fori_loop(0, chip_count, clear, 0)
    packed[pl.ds(tokens * pieces, pieces), :] = jnp.zeros((pieces, LANES), BF16)
    routes_copy.wait()
    gain_copy.wait()

    def take_part(first):
        groups = range(first, first + part, GROUP)
        for at in groups:
            square = jnp.zeros((GROUP, LANES), F32)
            for piece in range(pieces):
                values = columns_of(x, at, piece)
                square = square + values * values
            root_mean = jnp.sqrt(jnp.sum(square, axis=-1, keepdims=True) / width + EPSILON)
            inverses[pl.ds(at, GROUP), :] = jnp.broadcast_to(1.0 / root_mean, (GROUP, LANES))
        for at in groups:
            inverse = inverses[pl.ds(at, GROUP), :]
            for piece in range(pieces):
                unit = columns_of(x, at, piece) * inverse
                spread[pl.ds((at - first) * pieces + piece, GROUP, stride=pieces), :] = (
                    unit * gain_row[:, piece * LANES : (piece + 1) * LANES]
                )
        packed[first * pieces : (first + part) * pieces, :] = spread[...].astype(BF16)
        for token in range(first, first + part):
            experts = [routes[k, token] for k in range(top)]
            wheres = [count[expert] for expert in experts]
            for k in range(top):
                count[experts[k]] = wheres[k] + pieces
                place[k, token] = wheres[k]
                table[wheres[k] >> shift] = token

    for i in range(in_parts):
        copies[i].wait()
        take_part(i * part)
    sent = [
        pltpu.make_async_copy(place, place_out, out_sems.at[out_parts]),
        pltpu.make_async_copy(inverses, inverse_out, out_sems.at[out_parts + 1]),
    ]
    for copy in sent:
        copy.start()
    step = peers // out_parts

    def fill(pair, carry):
        for i in range(2):
            peer = pair * 2 + i
            chosen = [table[peer * slots + slot] for slot in range(slots)]
            for slot in range(slots):
                staged[peer, slot * pieces : (slot + 1) * pieces, :] = packed[
                    token_rows(chosen[slot], pieces), :
                ]
        return carry

    for i in range(out_parts):
        lax.fori_loop(i * step // 2, (i + 1) * step // 2, fill, 0)
        cut = pl.ds(i * step, step)
        sent.append(pltpu.make_async_copy(staged.at[cut], out.at[cut], out_sems.at[i]))
        sent[-1].start()
    for copy in sent:
        copy.wait()


def send_grads_kernel(place, weights, out_grad, out, rows):
    tokens, width = out_grad.shape
    pieces = width // LANES
    top = place.shape[0]
    zero_fill(out, pieces * top)

    def spread(group, carry):
        first = pl.multiple_of(group * GROUP, GROUP)
        for piece in range(pieces):
            rows[strip(group, piece, pieces), :] = columns_of(out_grad, first, piece)
        return carry

    lax.fori_loop(0, tokens // GROUP, spread, 0)

    def place_token(token, carry):
        row = rows[token_rows(token, pieces), :]
        for k in range(top):
            out[slot_rows(place[k, token], pieces), :] = (row * weights[k, token]).astype(BF16)
        return carry

    lax.fori_loop(0, tokens, place_token, 0)


def outputs_kernel(place, weights, layer_in, out_grad, returned, layer_out, gate_grad, rows, sums, dots):
    tokens, width = out_grad.shape
    pieces = width // LANES
    top = place.shape[0]

    def spread(group, carry):
        first = pl.multiple_of(group * GROUP, GROUP)
        for piece in range(pieces):
            rows[strip(group, piece, pieces), :] = columns_of(out_grad, first, piece)
        return carry

    lax.fori_loop(0, tokens // GROUP, spread, 0)

    def combine(token, carry):
        grad = rows[token_rows(token, pieces), :]
        total = jnp.zeros((pieces, LANES), F32)
        for k in range(top):
            row = returned[slot_rows(place[k, token], pieces), :].astype(F32)
            total = total + weights[k, token] * row
            dots[k, pl.ds(token, 1), :] = jnp.sum(row * grad, axis=0, keepdims=True)
        sums[token_rows(token, pieces), :] = total
        return carry

    lax.fori_loop(0, tokens, combine, 0)
    for k in range(top):
        gate_grad[k : k + 1, :] = jnp.sum(dots[k].T, axis=0, keepdims=True)

    def finish(group, carry):
        first = pl.multiple_of(group * GROUP, GROUP)
        for piece in range(pieces):
            x = columns_of(layer_in, first, piece)
            layer_out[pl.ds(first, GROUP), piece * LANES : (piece + 1) * LANES] = (
                x + sums[strip(group, piece, pieces), :]
            ).astype(BF16)
        return carry

    lax.fori_loop(0, tokens // GROUP, finish, 0)


def input_grad_kernel(
    place_in, x, inverse, gain_rows, grad, returned, input_grad, gain_grad,
    place, held, extra, units, sums, dots, result, place_sem, sems, extra_sem, out_sems,
):
    tokens, width = grad.shape
    pieces = width // LANES
    top = place.shape[0]
    peers, pairs = returned.shape[:2]
    share = gain_grad.shape[1]
    body_rows = (pairs - 1) * PAIR
    arrived = returned.reshape(peers, pairs * PAIR, LANES)
    parts = sems.shape[0]
    step = peers // parts
    blocks = held.reshape(peers, body_rows, LANES)
    copies = []
    for i in range(parts):
        cut = pl.ds(i * step, step)
        copies.append(
            pltpu.make_async_copy(arrived.at[cut, pl.ds(0, body_rows)], blocks.at[cut], sems.at[i])
        )
    copies.append(pltpu.make_async_copy(place_in, place, place_sem))
    copies.append(pltpu.make_async_copy(returned.at[:, pl.ds(pairs - 1, 1)], extra, extra_sem))
    for copy in copies:
        copy.start()

    def spread(group, carry):
        first = pl.multiple_of(group * GROUP, GROUP)
        scale = inverse[pl.ds(first, GROUP), :]
        for piece in range(pieces):
            units[strip(group, piece, pieces), :] = columns_of(x, first, piece) * scale
        return carry

    lax.fori_loop(0, tokens // GROUP, spread, 0)
    for copy in copies:
        copy.wait()

    def combine(block, carry):
        for i in range(8):
            token = block * 8 + i
            wheres = [place[k, token] for k in range(top)]
            total = jnp.zeros((pieces, LANES), F32)
            for where in wheres:
                total = total + held[slot_rows(where, pieces), :].astype(F32)
            q = total * gain_rows[...]
            sums[token_rows(token, pieces), :] = q
            along = q * units[token_rows(token, pieces), :]
            dots[pl.ds(token, 1), :] = jnp.sum(along, axis=0, keepdims=True)
        return carry

    lax.fori_loop(0, tokens // 8, combine, 0)
    dots[...] = inverse[...] * (jnp.sum(dots[...], axis=-1, keepdims=True) / width)

    def finish(group, carry):
        first = pl.multiple_of(group * GROUP, GROUP)
        scale = inverse[pl.ds(first, GROUP), :]
        lean = dots[pl.ds(first, GROUP), :]
        for piece in range(pieces):
            cut = slice(piece * LANES, (piece + 1) * LANES)
            q = sums[strip(group, piece, pieces), :]
            result[pl.ds(first, GROUP), cut] = (
                columns_of(grad, first, piece) + (q - columns_of(x, first, piece) * lean) * scale
            ).astype(BF16)
        return carry

    def add_peers(block, total):
        for i in range(8):
            total = total + extra[block * 8 + i, 0].astype(F32)
        return total

    out_parts = out_sems.shape[0]
    part = tokens // out_parts
    sent = []
    for i in range(out_parts):
        lax.fori_loop(i * part // GROUP, (i + 1) * part // GROUP, finish, 0)
        cut = pl.ds(i * part, part)
        sent.append(pltpu.make_async_copy(result.at[cut], input_grad.at[cut], out_sems.at[i]))
        sent[i].start()
    total = lax.fori_loop(0, peers // 8, add_peers, jnp.zeros((PAIR, LANES), F32))[0:1]
    gain_grad[...] = (
        total[:, :share] + total[:, share : 2 * share] + total[:, 2 * share : 3 * share]
    )
    for copy in sent:
        copy.wait()


def transposed(left, right):
    return lax.dot_general(left, right, (((1,), (1,)), ((), ())), preferred_element_type=F32)


def exchange(buffer):
    return lax.all_to_all(buffer, ("dev", "role"), split_axis=0, concat_axis=0, tiled=True)


def three_parts(values):
    high = lax.reduce_precision(values, 8, 7)
    middle = lax.reduce_precision(values - high, 8, 7)
    low = values - high - middle
    return high.astype(BF16), middle.astype(BF16), low.astype(BF16)


def body(layer_in, norm_gain, routes, gate_weights, out_grad, expert_gate_up, expert_down):
    tokens, width = layer_in.shape
    top = routes.shape[1]
    peers = lax.axis_size(AXES)
    slots = tokens * top * 5 // (4 * peers)
    pieces = width // LANES
    chips = lax.axis_size("dev")
    hidden_units = expert_down.shape[1]
    row_count = peers * slots
    block = (peers, slots * pieces, LANES)
    gain = norm_gain.reshape(1, width)
    by_choice = routes.T
    weights = gate_weights.T
    token_scratch = pltpu.VMEM((tokens * pieces, LANES), F32)

    in_parts, out_parts = 4, 8
    send_rows, place, inverse = pl.pallas_call(
        functools.partial(send_rows_kernel, chips),
        out_shape=(
            jax.ShapeDtypeStruct(block, BF16),
            jax.ShapeDtypeStruct((top, tokens), jnp.int32),
            jax.ShapeDtypeStruct((tokens, LANES), F32),
        ),
        in_specs=[HBM, HBM, HBM],
        out_specs=(HBM, HBM, HBM),
        scratch_shapes=[
            pltpu.SMEM((top, tokens), jnp.int32),
            pltpu.VMEM((tokens, width), BF16),
            pltpu.VMEM((1, width), F32),
            pltpu.VMEM((tokens // in_parts * pieces, LANES), F32),
            pltpu.VMEM(((tokens + 1) * pieces, LANES), BF16),
            pltpu.VMEM(block, BF16),
            pltpu.VMEM((tokens, LANES), F32),
            pltpu.SMEM((top, tokens), jnp.int32),
            pltpu.SMEM((peers,), jnp.int32),
            pltpu.SMEM((row_count,), jnp.int32),
            pltpu.SemaphoreType.DMA((in_parts + 2,)),
            pltpu.SemaphoreType.DMA((out_parts + 2,)),
        ],
        compiler_params=WHOLE,
        name="send_rows",
    )(by_choice, layer_in, gain)
    arrived = exchange(send_rows).reshape(row_count, pieces, LANES).reshape(row_count, width)

    send_grads = pl.pallas_call(
        send_grads_kernel,
        out_shape=jax.ShapeDtypeStruct((row_count * pieces, LANES), BF16),
        in_specs=[SMEM, SMEM, VMEM],
        out_specs=VMEM,
        scratch_shapes=[token_scratch],
        compiler_params=PARAMS,
        name="send_grads",
    )(place, weights, out_grad)
    grad_rows = exchange(send_grads.reshape(block)).reshape(row_count, pieces, LANES).reshape(row_count, width)

    w_gate_up = expert_gate_up[0]
    w_down = expert_down[0]
    projected = jnp.dot(arrived, w_gate_up, preferred_element_type=F32)
    g = projected[:, :hidden_units]
    u = projected[:, hidden_units:]
    s = jax.nn.sigmoid(g)
    active = g * s
    hidden = (active * u).astype(BF16)
    expert_rows = jnp.dot(hidden, w_down, preferred_element_type=F32).astype(BF16)
    returned = exchange(expert_rows.reshape(row_count, pieces, LANES).reshape(block))

    hidden_grad = transposed(grad_rows, w_down)
    gate_part = hidden_grad * u * s * (1.0 + g * (1.0 - s))
    pre_grad = jnp.concatenate([gate_part, hidden_grad * active], axis=-1).astype(BF16)
    back_rows = transposed(pre_grad, w_gate_up).astype(BF16)
    terms = jnp.sum(back_rows.astype(F32) * arrived.astype(F32), axis=0) / norm_gain
    share = width // peers
    parts = jnp.concatenate(
        [
            jnp.swapaxes(p.reshape(peers // chips, chips, share), 0, 1).reshape(peers, share)
            for p in three_parts(terms)
        ],
        axis=-1,
    )
    parts = jnp.pad(parts[:, None, None, :], ((0, 0), (0, 0), (0, PAIR - 1), (0, LANES - 3 * share)))
    back_pairs = back_rows.reshape(row_count, pieces, LANES).reshape(peers, -1, PAIR, LANES)
    send_back = jnp.concatenate([back_pairs, parts], axis=1)
    came_back = exchange(send_back)

    layer_out, gate_grad = pl.pallas_call(
        outputs_kernel,
        out_shape=(
            jax.ShapeDtypeStruct((tokens, width), BF16),
            jax.ShapeDtypeStruct((top, tokens), F32),
        ),
        in_specs=[SMEM, SMEM, VMEM, VMEM, VMEM],
        out_specs=(VMEM, VMEM),
        scratch_shapes=[token_scratch, token_scratch, pltpu.VMEM((top, tokens, LANES), F32)],
        compiler_params=SMALL,
        name="outputs",
    )(place, weights, layer_in, out_grad, returned.reshape(row_count * pieces, LANES))

    input_grad, gain_grad = pl.pallas_call(
        input_grad_kernel,
        out_shape=(
            jax.ShapeDtypeStruct((tokens, width), BF16),
            jax.ShapeDtypeStruct((1, share), F32),
        ),
        in_specs=[HBM, VMEM, VMEM, VMEM, VMEM, HBM],
        out_specs=(HBM, VMEM),
        scratch_shapes=[
            pltpu.SMEM((top, tokens), jnp.int32),
            pltpu.VMEM((row_count * pieces, LANES), BF16),
            pltpu.VMEM((peers, 1, PAIR, LANES), BF16),
            token_scratch,
            token_scratch,
            pltpu.VMEM((tokens, LANES), F32),
            pltpu.VMEM((tokens, width), BF16),
            pltpu.SemaphoreType.DMA(()),
            pltpu.SemaphoreType.DMA((8,)),
            pltpu.SemaphoreType.DMA(()),
            pltpu.SemaphoreType.DMA((8,)),
        ],
        compiler_params=SMALL,
        name="input_grad",
    )(place, layer_in, inverse, norm_gain.reshape(pieces, LANES), out_grad, came_back)
    gain_grad = gain_grad.reshape(share)
    return (layer_out, input_grad, gate_grad.T, gain_grad)


def solution(mesh):
    split = P(AXES, None)
    in_specs = (split, P(), split, split, split, P(AXES, None, None), P(AXES, None, None))
    out_specs = (split, split, split, P(AXES))
    return jax.shard_map(body, mesh=mesh, in_specs=in_specs, out_specs=out_specs, check_vma=False)
```
